32 devices in a mesh: row: 4 (over y, core), col: 8 (over z, x).
Axes of the slice: x: 2, y: 2, z: 4, core: 2. Of those that a mesh axis runs over, the one named last changes fastest.
Arguments:
- trailing_inverse: float32 [6144, 6144], P('row', 'col'), may hold values from -6 to 6
- factor_cols: float32 [3, 6144, 256], P(None, ('col', 'row')), may hold values from -0.078125 to 0.078125
- factor_blocks: float32 [3, 256, 256], replicated, may hold values from -0.375 to 0.375
- diag_inverse: float32 [3, 256, 256], replicated, may hold values from -6 to 6
Outputs:
- inv_cols: float32 [3, 6144, 256], P(None, ('row', 'col'))
- inv_diag: float32 [3, 256, 256], replicated
- inv_cross: float32 [3, 256, 256], replicated
The draws below stay inside these ranges and needn't reach their ends.
All inputs are finite; a program needn't handle non-finite values.
Results may differ from the reference program's by a relative error of at most 0.0001.
Values sent between devices are 32-bit elements; how exact they have to be, the bound alone decides.
A program may use at most 128 MiB of HBM per device.

```python
import jax
import jax.numpy as jnp
from jax import lax

W = 256
NS = 3
R = 6144
NPAIR = 3


def levels(own_key, shape, cuts, low, largest):
    gain = 1.0
    for axis_at, parts in cuts:
        draws = jax.random.uniform(jax.random.fold_in(jax.random.fold_in(own_key, 6), axis_at), (parts,), jnp.float32, low / len(cuts), largest / len(cuts))
        gain = gain * jnp.repeat(jnp.exp(draws), shape[axis_at] // parts).reshape((-1,) + (1,) * (len(shape) - 1 - axis_at))
    return gain


def bell_draw(key, extent, spread, limit, shards=(), dtype=jnp.bfloat16):
    array = spread * jax.random.normal(key, extent, jnp.float32)
    if shards:
        array = array * levels(key, extent, shards, -0.22, 0.18)
    return jnp.clip(array, -limit, limit).astype(dtype)


def setup_inputs(seed: int = 0) -> dict:
    key_list = jax.random.split(jax.random.key(seed), 5)
    trailing_inverse = bell_draw(key_list[0], (R, R), 1.0, 6.0, ((0, 4), (1, 8)), jnp.float32)
    factor_cols = bell_draw(key_list[1], (NS, R, W), R ** -0.5, 0.078125, ((1, 32),), jnp.float32)
    factor_blocks = bell_draw(key_list[2], (NPAIR, W, W), W ** -0.5, 0.375, (), jnp.float32)
    diag_inverse = bell_draw(key_list[3], (NS, W, W), 1.0, 6.0, (), jnp.float32)
    return dict(trailing_inverse=trailing_inverse, factor_cols=factor_cols, factor_blocks=factor_blocks, diag_inverse=diag_inverse)


def product(left, right):
    return jnp.dot(left, right, precision=lax.Precision.HIGHEST, preferred_element_type=jnp.float32)


def pair_order(node_count):
    return [(later_node, target_node) for target_node in reversed(range(node_count)) for later_node in range(target_node + 1, node_count)]


def reference(trailing_inverse, factor_cols, factor_blocks, diag_inverse):
    node_count = factor_cols.shape[0]
    pair_list = pair_order(node_count)
    columns = [None] * node_count
    blocks = {}
    for target_node in reversed(range(node_count)):
        accumulated = product(trailing_inverse, factor_cols[target_node])
        for later_node in range(target_node + 1, node_count):
            accumulated = accumulated + product(columns[later_node], factor_blocks[pair_list.index((later_node, target_node))])
        columns[target_node] = -accumulated
        for later_node in range(target_node + 1, node_count):
            value_sum = product(columns[later_node].T, factor_cols[target_node])
            for other_node in range(target_node + 1, node_count):
                if later_node >= other_node:
                    block_value = blocks[(later_node, other_node)]
                else:
                    block_value = blocks[(other_node, later_node)].T
                value_sum = value_sum + product(block_value, factor_blocks[pair_list.index((other_node, target_node))])
            blocks[(later_node, target_node)] = -value_sum
        diag_term = product(factor_cols[target_node].T, columns[target_node])
        for later_node in range(target_node + 1, node_count):
            diag_term = diag_term + product(factor_blocks[pair_list.index((later_node, target_node))].T, blocks[(later_node, target_node)])
        blocks[(target_node, target_node)] = diag_inverse[target_node] - diag_term
    inv_cols = jnp.stack(columns)
    inv_diag = jnp.stack([blocks[(node_index, node_index)] for node_index in range(node_count)])
    inv_cross = jnp.stack([blocks[slot_pair] for slot_pair in pair_list])
    return (inv_cols, inv_diag, inv_cross)
```

```python
import functools

import jax
import jax.numpy as jnp
from jax import lax
from jax.experimental import pallas as pl
from jax.experimental.pallas import tpu as pltpu
from jax.sharding import PartitionSpec as P

MESH = pl.DeviceIdType.MESH
CORES = 2


def exact_dot(left, right, left_dim=1):
    return lax.dot_general(
        left,
        right,
        (((left_dim,), (0,)), ((), ())),
        precision=lax.Precision.HIGHEST,
        preferred_element_type=jnp.float32,
    )


def split(value):
    high = value.astype(jnp.bfloat16)
    low = (value - high.astype(jnp.float32)).astype(jnp.bfloat16)
    return high, low


def pair_order(node_count):
    return [
        (later_node, target_node)
        for target_node in reversed(range(node_count))
        for later_node in range(target_node + 1, node_count)
    ]


def row_splits(rows, row_count, col_count):
    splits = row_count
    while splits > 1 and rows % (splits * col_count * 8):
        splits //= 2
    return splits


def kernel(
    sizes,
    t_hbm,
    f_ref,
    b_ref,
    d_ref,
    v_ref,
    diag_ref,
    cross_ref,
    t_ref,
    fg,
    fh,
    fl,
    g,
    xr,
    zr,
    fown,
    *rest,
):
    row_count, col_count, nx, ny, nz, nodes, piece, width = sizes
    stages = [rest[0:4], rest[4:8]]
    send_sem, recv_sem, t_sem = rest[8:]
    r = lax.axis_index("row")
    c = lax.axis_index("col")
    y, core = r // CORES, r % CORES
    z, x = c // nx, c % nx
    total = row_count * col_count
    me = r * col_count + c
    pairs = pair_order(nodes)

    t_copy = pltpu.make_async_copy(t_hbm, t_ref, t_sem)
    t_copy.start()

    barrier = pltpu.get_barrier_semaphore()

    def greet(step, carry):
        other = (me + step) % total
        pl.semaphore_signal(
            barrier, inc=1, device_id=(other // col_count, other % col_count), device_id_type=MESH
        )
        return carry

    lax.fori_loop(1, total, greet, 0)
    pl.semaphore_wait(barrier, total - 1)

    def remote(src, dst, sem, row, col):
        return pltpu.make_async_remote_copy(
            src_ref=src,
            dst_ref=dst,
            send_sem=send_sem.at[sem],
            recv_sem=recv_sem.at[sem],
            device_id=(row, col),
            device_id_type=MESH,
        )

    order = list(reversed(range(nodes)))
    base = 0
    started = []
    sibling = y * CORES + 1 - core

    def rows_of(row):
        return pl.ds(pl.multiple_of(row * piece, 8), piece)

    across, inside, relayed = {}, {}, {}
    for node in order:
        for dy in range(1, ny):
            target = ((y + dy) % ny) * CORES + core
            across[node, dy] = remote(f_ref.at[node], fg.at[node, rows_of(r)], base, target, c)
            base += 1
            source = ((y - dy + ny) % ny) * CORES + core
            landed = fg.at[node, rows_of(source)]
            relayed[node, dy] = remote(landed, landed, base, sibling, c)
            base += 1
        inside[node] = remote(f_ref.at[node], fg.at[node, rows_of(r)], base, sibling, c)
        base += 1
    for node in order:
        for dy in range(1, ny):
            across[node, dy].start()
        inside[node].start()

    place = c * row_count + r
    own_row, own_col = place // col_count, place % col_count
    stays = place == me
    owned = remote(f_ref, fown, base, own_row, own_col)
    base += 1

    @pl.when(jnp.logical_not(stays))
    def _():
        owned.start()

    @pl.when(stays)
    def _():
        fown[...] = f_ref[...]

    x_base = base
    base += nodes * nz * (nx - 1)

    def x_copy(node, dz, dx):
        target = (x + dx) % nx
        return remote(
            g.at[node, dz, rows_of(target)],
            xr.at[node, dz, dx - 1],
            x_base + (node * nz + dz) * (nx - 1) + dx - 1,
            r,
            z * nx + target,
        )

    for node in order:
        fg[node, rows_of(r)] = f_ref[node]
    t_copy.wait()
    for node in order:
        for dy in range(1, ny):
            across[node, dy].wait_recv()
            relayed[node, dy].start()
        inside[node].wait_recv()
        for dy in range(1, ny):
            relayed[node, dy].wait_recv()
        high, low = split(fg[node])
        fh[...] = high
        fl[...] = low

        def produce(dz, carry):
            target = (z + dz + 1) % nz
            start = target * (nx * piece)
            span = min(nx, CORES) * piece
            for at in range(0, nx * piece, span):
                rows = pl.ds(pl.multiple_of(start + at, 8), span)
                t_high, t_low = split(t_ref[rows])
                value = jnp.dot(t_high, fh[...], preferred_element_type=jnp.float32)
                value += jnp.dot(t_low, fh[...], preferred_element_type=jnp.float32)
                value += jnp.dot(t_high, fl[...], preferred_element_type=jnp.float32)
                g[node, dz, at : at + span] = value
            for dx in range(1, nx):
                x_copy(node, dz, dx).start()
            return carry

        lax.fori_loop(0, nz, produce, 0)

    z_base = base
    base += nodes * (nz - 1)

    def z_copy(node, dz):
        target = (z + dz + 1) % nz
        return remote(
            g.at[node, dz, rows_of(x)],
            zr.at[node, dz],
            z_base + node * (nz - 1) + dz,
            r,
            target * nx + x,
        )

    def forward(node, dz):
        value = g[node, dz, rows_of(x)]
        for dx in range(1, nx):
            x_copy(node, dz, dx).wait_recv()
            value += xr[node, dz, dx - 1]
        g[node, dz, rows_of(x)] = value
        if dz < nz - 1:
            z_copy(node, dz).start()

    def finish(node):
        value = g[node, nz - 1, rows_of(x)]
        for dz in range(nz - 1):
            z_copy(node, dz).wait_recv()
            value += zr[node, dz]
        for later in range(node + 1, nodes):
            value += exact_dot(v_ref[later], b_ref[pairs.index((later, node))])
        v_ref[node] = -value

    class Total:
        def __init__(self, refs, sem):
            self.part, self.first, self.second, self.out = refs
            rows = self.part.shape[0]
            self.splits = row_splits(rows, row_count, col_count)
            self.share = rows // self.splits
            self.small = self.share // col_count
            self.sem = sem
            self.copies = []

        def share_of(self, row):
            return pl.ds(pl.multiple_of((row % self.splits) * self.share, 8), self.share)

        def small_of(self, col):
            start = (r % self.splits) * self.share + col * self.small
            return pl.ds(pl.multiple_of(start, 8), self.small)

        def send(self, src, dst, row, col):
            copy = remote(src, dst, self.sem, row, col)
            self.sem += 1
            copy.start()
            started.append(copy)
            self.copies.append(copy)

        def receive(self):
            for copy in self.copies:
                copy.wait_recv()
            self.copies = []

        def step1(self):
            for dr in range(1, row_count):
                row = (r + dr) % row_count
                self.send(self.part.at[self.share_of(row)], self.first.at[r], row, c)
            self.first[r] = self.part[self.share_of(r)]

        def step2(self):
            self.receive()
            value = self.first[0]
            for row in range(1, row_count):
                value += self.first[row]
            self.part[self.share_of(r)] = value
            for dc in range(1, col_count):
                col = (c + dc) % col_count
                self.send(self.part.at[self.small_of(col)], self.second.at[c], r, col)
            self.second[c] = self.part[self.small_of(c)]

        def step3(self):
            self.receive()
            value = self.second[0]
            for col in range(1, col_count):
                value += self.second[col]
            self.out[self.small_of(c)] = value
            for dc in range(1, col_count):
                ref = self.out.at[self.small_of(c)]
                self.send(ref, ref, r, (c + dc) % col_count)

        def step4(self):
            self.receive()
            group = (r // self.splits) * self.splits
            for dr in range(1, self.splits):
                ref = self.out.at[self.share_of(r)]
                self.send(ref, ref, group + (r - group + dr) % self.splits, c)

    per_total = 2 * (row_count - 1) + 2 * (col_count - 1)
    many, last = Total(stages[0], base), Total(stages[1], base + per_total)

    def block(ref, index):
        return ref.at[index * width : (index + 1) * width]

    slots = {}
    early = []
    for node in order[:-1]:
        slots[node, node] = len(early)
        early.append((node, node))
        for target in reversed(range(node)):
            slots[node, target] = len(early)
            early.append((node, target))

    for node in order[:-1]:
        for dz in range(nz):
            forward(node, dz)

    @pl.when(jnp.logical_not(stays))
    def _():
        owned.wait()

    def contribute(node):
        block(many.part, slots[node, node])[...] = exact_dot(fown[node], v_ref[node], 0)
        for target in reversed(range(node)):
            block(many.part, slots[node, target])[...] = exact_dot(v_ref[node], fown[target], 0)

    for node in order[:-2]:
        finish(node)
        contribute(node)
    for dz in range(nz - 1):
        forward(0, dz)
    if nodes > 1:
        finish(1)
        contribute(1)
        many.step1()
    forward(0, nz - 1)
    many.step2()
    finish(0)
    last.part[...] = exact_dot(fown[0], v_ref[0], 0)
    last.step1()
    many.step3()
    last.step2()
    many.step4()
    last.step3()
    many.receive()

    for node in order:
        for later in range(node + 1, nodes):
            value = block(many.out, slots[later, node])[...]
            for other in range(node + 1, nodes):
                factor = b_ref[pairs.index((other, node))]
                if later == other:
                    value += exact_dot(diag_ref[other], factor)
                elif later > other:
                    value += exact_dot(cross_ref[pairs.index((later, other))], factor)
                else:
                    value += exact_dot(cross_ref[pairs.index((other, later))], factor, 0)
            cross_ref[pairs.index((later, node))] = -value
        value = d_ref[node]
        if node > 0:
            value -= block(many.out, slots[node, node])[...]
        for later in range(node + 1, nodes):
            pair = pairs.index((later, node))
            value -= exact_dot(b_ref[pair], cross_ref[pair], 0)
        diag_ref[node] = value
    last.step4()
    last.receive()
    diag_ref[0] = diag_ref[0] - last.out[...]

    for copy in started:
        copy.wait_send()
    for node in order:
        for dy in range(1, ny):
            across[node, dy].wait_send()
            relayed[node, dy].wait_send()
        inside[node].wait_send()
        for dz in range(nz):
            for dx in range(1, nx):
                x_copy(node, dz, dx).wait_send()
            if dz < nz - 1:
                z_copy(node, dz).wait_send()


def per_device(trailing_inverse, factor_cols, factor_blocks, diag_inverse):
    nodes, piece, width = factor_cols.shape
    row_count = lax.axis_size("row")
    col_count = lax.axis_size("col")
    ny = row_count // CORES
    nx = ny if col_count % ny == 0 else 1
    nz = col_count // nx
    depth = trailing_inverse.shape[1]
    sizes = (row_count, col_count, nx, ny, nz, nodes, piece, width)
    pair_count = factor_blocks.shape[0]

    def f32(*shape):
        return pltpu.VMEM(shape, jnp.float32)

    def total_refs(blocks):
        rows = blocks * width
        share = rows // row_splits(rows, row_count, col_count)
        return [
            f32(rows, width),
            f32(row_count, share, width),
            f32(col_count, share // col_count, width),
            f32(rows, width),
        ]

    early = pair_count + nodes - 1
    copies = (
        nodes * (2 * (ny - 1) + 1)
        + 1
        + nodes * nz * (nx - 1)
        + nodes * (nz - 1)
        + 4 * (row_count - 1 + col_count - 1)
    )
    vmem = pl.BlockSpec(memory_space=pltpu.VMEM)
    return pl.pallas_call(
        functools.partial(kernel, sizes),
        out_shape=(
            jax.ShapeDtypeStruct((nodes, piece, width), jnp.float32),
            jax.ShapeDtypeStruct((nodes, width, width), jnp.float32),
            jax.ShapeDtypeStruct((pair_count, width, width), jnp.float32),
        ),
        in_specs=[pl.BlockSpec(memory_space=pl.ANY), vmem, vmem, vmem],
        out_specs=(vmem, vmem, vmem),
        scratch_shapes=[
            f32(*trailing_inverse.shape),
            f32(nodes, depth, width),
            pltpu.VMEM((depth, width), jnp.bfloat16),
            pltpu.VMEM((depth, width), jnp.bfloat16),
            f32(nodes, nz, nx * piece, width),
            f32(nodes, nz, max(nx - 1, 1), piece, width),
            f32(nodes, max(nz - 1, 1), piece, width),
            f32(nodes, piece, width),
            *total_refs(early),
            *total_refs(1),
            pltpu.SemaphoreType.DMA((copies,)),
            pltpu.SemaphoreType.DMA((copies,)),
            pltpu.SemaphoreType.DMA,
        ],
        compiler_params=pltpu.CompilerParams(
            collective_id=0, has_side_effects=True, vmem_limit_bytes=61 * 1024 * 1024
        ),
    )(trailing_inverse, factor_cols, factor_blocks, diag_inverse)


def solution(mesh):
    return jax.shard_map(
        per_device,
        mesh=mesh,
        in_specs=(P("row", "col"), P(None, ("col", "row"), None), P(), P()),
        out_specs=(P(None, ("row", "col"), None), P(), P()),
        check_vma=False,
    )
```

```python
import functools

import jax
import jax.numpy as jnp
from jax import lax
from jax.experimental import pallas as pl
from jax.experimental.pallas import tpu as pltpu
from jax.sharding import PartitionSpec as P

MESH = pl.DeviceIdType.MESH
CORES = 2


def split(value):
    high = value.astype(jnp.bfloat16)
    low = (value - high.astype(jnp.float32)).astype(jnp.bfloat16)
    return high, low


def exact_dot(left, right, left_dim=1):
    left_high, left_low = split(left)
    right_high, right_low = split(right)
    value = None
    for one, two in ((left_high, right_high), (left_low, right_high), (left_high, right_low)):
        term = lax.dot_general(
            one, two, (((left_dim,), (0,)), ((), ())), preferred_element_type=jnp.float32
        )
        value = term if value is None else value + term
    return value


def pair_order(node_count):
    return [
        (later_node, target_node)
        for target_node in reversed(range(node_count))
        for later_node in range(target_node + 1, node_count)
    ]


def row_splits(rows, row_count, col_count):
    splits = row_count
    while splits > 1 and rows % (splits * col_count * 8):
        splits //= 2
    return splits


def kernel(
    sizes,
    t_hbm,
    f_ref,
    b_ref,
    d_ref,
    v_ref,
    diag_ref,
    cross_ref,
    t_ref,
    fg,
    fh,
    fl,
    g,
    xr,
    zr,
    fown,
    *rest,
):
    row_count, col_count, nx, ny, nz, nodes, piece, width = sizes
    stages = [rest[0:4], rest[4:8]]
    send_sem, recv_sem, t_sem = rest[8:]
    r = lax.axis_index("row")
    c = lax.axis_index("col")
    y, core = r // CORES, r % CORES
    z, x = c // nx, c % nx
    total = row_count * col_count
    me = r * col_count + c
    pairs = pair_order(nodes)

    t_copy = pltpu.make_async_copy(t_hbm, t_ref, t_sem)
    t_copy.start()

    barrier = pltpu.get_barrier_semaphore()

    def greet(step, carry):
        other = (me + step) % total
        pl.semaphore_signal(
            barrier, inc=1, device_id=(other // col_count, other % col_count), device_id_type=MESH
        )
        return carry

    lax.fori_loop(1, total, greet, 0)
    pl.semaphore_wait(barrier, total - 1)

    def remote(src, dst, sem, row, col):
        return pltpu.make_async_remote_copy(
            src_ref=src,
            dst_ref=dst,
            send_sem=send_sem.at[sem],
            recv_sem=recv_sem.at[sem],
            device_id=(row, col),
            device_id_type=MESH,
        )

    order = list(reversed(range(nodes)))
    base = 0
    started = []
    sibling = y * CORES + 1 - core

    def rows_of(row):
        return pl.ds(pl.multiple_of(row * piece, 8), piece)

    across, inside, relayed = {}, {}, {}
    for node in order:
        for dy in range(1, ny):
            target = ((y + dy) % ny) * CORES + core
            across[node, dy] = remote(f_ref.at[node], fg.at[node, rows_of(r)], base, target, c)
            base += 1
            source = ((y - dy + ny) % ny) * CORES + core
            landed = fg.at[node, rows_of(source)]
            relayed[node, dy] = remote(landed, landed, base, sibling, c)
            base += 1
        inside[node] = remote(f_ref.at[node], fg.at[node, rows_of(r)], base, sibling, c)
        base += 1
    for node in order:
        for dy in range(1, ny):
            across[node, dy].start()
        inside[node].start()

    place = c * row_count + r
    own_row, own_col = place // col_count, place % col_count
    stays = place == me
    owned = remote(f_ref, fown, base, own_row, own_col)
    base += 1

    @pl.when(jnp.logical_not(stays))
    def _():
        owned.start()

    @pl.when(stays)
    def _():
        fown[...] = f_ref[...]

    x_base = base
    base += nodes * nz * (nx - 1)

    def x_copy(node, dz, dx):
        target = (x + dx) % nx
        return remote(
            g.at[node, dz, rows_of(target)],
            xr.at[node, dz, dx - 1],
            x_base + (node * nz + dz) * (nx - 1) + dx - 1,
            r,
            z * nx + target,
        )

    for node in order:
        fg[node, rows_of(r)] = f_ref[node]
    t_copy.wait()
    for node in order:
        for dy in range(1, ny):
            across[node, dy].wait_recv()
            relayed[node, dy].start()
        inside[node].wait_recv()
        for dy in range(1, ny):
            relayed[node, dy].wait_recv()
        high, low = split(fg[node])
        fh[...] = high
        fl[...] = low

        def produce(dz, carry):
            target = (z + dz + 1) % nz
            start = target * (nx * piece)
            span = min(nx, CORES) * piece
            for at in range(0, nx * piece, span):
                rows = pl.ds(pl.multiple_of(start + at, 8), span)
                t_high, t_low = split(t_ref[rows])
                value = jnp.dot(t_high, fh[...], preferred_element_type=jnp.float32)
                value += jnp.dot(t_low, fh[...], preferred_element_type=jnp.float32)
                value += jnp.dot(t_high, fl[...], preferred_element_type=jnp.float32)
                g[node, dz, at : at + span] = value
            for dx in range(1, nx):
                x_copy(node, dz, dx).start()
            return carry

        lax.fori_loop(0, nz, produce, 0)

    z_base = base
    base += nodes * (nz - 1)

    def z_copy(node, dz):
        target = (z + dz + 1) % nz
        return remote(
            g.at[node, dz, rows_of(x)],
            zr.at[node, dz],
            z_base + node * (nz - 1) + dz,
            r,
            target * nx + x,
        )

    def forward(node, dz):
        value = g[node, dz, rows_of(x)]
        for dx in range(1, nx):
            x_copy(node, dz, dx).wait_recv()
            value += xr[node, dz, dx - 1]
        g[node, dz, rows_of(x)] = value
        if dz < nz - 1:
            z_copy(node, dz).start()

    def finish(node):
        value = g[node, nz - 1, rows_of(x)]
        for dz in range(nz - 1):
            z_copy(node, dz).wait_recv()
            value += zr[node, dz]
        for later in range(node + 1, nodes):
            value += exact_dot(v_ref[later], b_ref[pairs.index((later, node))])
        v_ref[node] = -value

    class Total:
        def __init__(self, refs, sem):
            self.part, self.first, self.second, self.out = refs
            rows = self.part.shape[0]
            self.splits = row_splits(rows, row_count, col_count)
            self.share = rows // self.splits
            self.small = self.share // col_count
            self.sem = sem
            self.copies = []

        def share_of(self, row):
            return pl.ds(pl.multiple_of((row % self.splits) * self.share, 8), self.share)

        def small_of(self, col):
            start = (r % self.splits) * self.share + col * self.small
            return pl.ds(pl.multiple_of(start, 8), self.small)

        def send(self, src, dst, row, col):
            copy = remote(src, dst, self.sem, row, col)
            self.sem += 1
            copy.start()
            started.append(copy)
            self.copies.append(copy)

        def receive(self):
            for copy in self.copies:
                copy.wait_recv()
            self.copies = []

        def step1(self):
            for dr in range(1, row_count):
                row = (r + dr) % row_count
                self.send(self.part.at[self.share_of(row)], self.first.at[r], row, c)
            self.first[r] = self.part[self.share_of(r)]

        def step2(self):
            self.receive()
            value = self.first[0]
            for row in range(1, row_count):
                value += self.first[row]
            self.part[self.share_of(r)] = value
            for dc in range(1, col_count):
                col = (c + dc) % col_count
                self.send(self.part.at[self.small_of(col)], self.second.at[c], r, col)
            self.second[c] = self.part[self.small_of(c)]

        def step3(self):
            self.receive()
            value = self.second[0]
            for col in range(1, col_count):
                value += self.second[col]
            self.out[self.small_of(c)] = value
            for dc in range(1, col_count):
                ref = self.out.at[self.small_of(c)]
                self.send(ref, ref, r, (c + dc) % col_count)

        def step4(self):
            self.receive()
            self.pass_on = []
            group = (r // self.splits) * self.splits
            ref = self.out.at[self.share_of(r)]
            near = group + (r - group) // CORES * CORES + 1 - core
            for step in range(CORES, self.splits, CORES):
                ahead = group + (r - group + step) % self.splits
                self.send(ref, ref, ahead, c)
                behind = group + (r - group - step + self.splits) % self.splits
                self.pass_on.append((self.copies.pop(), behind))
            if self.splits > 1:
                self.send(ref, ref, near, c)

        def step5(self):
            for copy, row in self.pass_on:
                copy.wait_recv()
                ref = self.out.at[self.share_of(row)]
                self.send(ref, ref, sibling, c)
            self.receive()

    per_total = 2 * (row_count - 1) + 2 * (col_count - 1)
    many, last = Total(stages[0], base), Total(stages[1], base + per_total)

    def block(ref, index):
        return ref.at[index * width : (index + 1) * width]

    slots = {}
    early = []
    for node in order[:-1]:
        slots[node, node] = len(early)
        early.append((node, node))
        for target in reversed(range(node)):
            slots[node, target] = len(early)
            early.append((node, target))

    for node in order[:-1]:
        for dz in range(nz):
            forward(node, dz)

    @pl.when(jnp.logical_not(stays))
    def _():
        owned.wait()

    def contribute(node):
        block(many.part, slots[node, node])[...] = exact_dot(fown[node], v_ref[node], 0)
        for target in reversed(range(node)):
            block(many.part, slots[node, target])[...] = exact_dot(v_ref[node], fown[target], 0)

    for node in order[:-2]:
        finish(node)
        contribute(node)
    for dz in range(nz - 1):
        forward(0, dz)
    if nodes > 1:
        finish(1)
        contribute(1)
        many.step1()
    forward(0, nz - 1)
    many.step2()
    finish(0)
    last.part[...] = exact_dot(fown[0], v_ref[0], 0)
    last.step1()
    many.step3()
    last.step2()
    many.step4()
    last.step3()
    many.step5()

    for node in order:
        for later in range(node + 1, nodes):
            value = block(many.out, slots[later, node])[...]
            for other in range(node + 1, nodes):
                factor = b_ref[pairs.index((other, node))]
                if later == other:
                    value += exact_dot(diag_ref[other], factor)
                elif later > other:
                    value += exact_dot(cross_ref[pairs.index((later, other))], factor)
                else:
                    value += exact_dot(cross_ref[pairs.index((other, later))], factor, 0)
            cross_ref[pairs.index((later, node))] = -value
        value = d_ref[node]
        if node > 0:
            value -= block(many.out, slots[node, node])[...]
        for later in range(node + 1, nodes):
            pair = pairs.index((later, node))
            value -= exact_dot(b_ref[pair], cross_ref[pair], 0)
        diag_ref[node] = value
    last.step4()
    last.step5()
    diag_ref[0] = diag_ref[0] - last.out[...]

    for copy in started:
        copy.wait_send()
    for node in order:
        for dy in range(1, ny):
            across[node, dy].wait_send()
            relayed[node, dy].wait_send()
        inside[node].wait_send()
        for dz in range(nz):
            for dx in range(1, nx):
                x_copy(node, dz, dx).wait_send()
            if dz < nz - 1:
                z_copy(node, dz).wait_send()


def per_device(trailing_inverse, factor_cols, factor_blocks, diag_inverse):
    nodes, piece, width = factor_cols.shape
    row_count = lax.axis_size("row")
    col_count = lax.axis_size("col")
    ny = row_count // CORES
    nx = ny if col_count % ny == 0 else 1
    nz = col_count // nx
    depth = trailing_inverse.shape[1]
    sizes = (row_count, col_count, nx, ny, nz, nodes, piece, width)
    pair_count = factor_blocks.shape[0]

    def f32(*shape):
        return pltpu.VMEM(shape, jnp.float32)

    def total_refs(blocks):
        rows = blocks * width
        share = rows // row_splits(rows, row_count, col_count)
        return [
            f32(rows, width),
            f32(row_count, share, width),
            f32(col_count, share // col_count, width),
            f32(rows, width),
        ]

    early = pair_count + nodes - 1
    copies = (
        nodes * (2 * (ny - 1) + 1)
        + 1
        + nodes * nz * (nx - 1)
        + nodes * (nz - 1)
        + 4 * (row_count - 1 + col_count - 1)
    )
    vmem = pl.BlockSpec(memory_space=pltpu.VMEM)
    return pl.pallas_call(
        functools.partial(kernel, sizes),
        out_shape=(
            jax.ShapeDtypeStruct((nodes, piece, width), jnp.float32),
            jax.ShapeDtypeStruct((nodes, width, width), jnp.float32),
            jax.ShapeDtypeStruct((pair_count, width, width), jnp.float32),
        ),
        in_specs=[pl.BlockSpec(memory_space=pl.ANY), vmem, vmem, vmem],
        out_specs=(vmem, vmem, vmem),
        scratch_shapes=[
            f32(*trailing_inverse.shape),
            f32(nodes, depth, width),
            pltpu.VMEM((depth, width), jnp.bfloat16),
            pltpu.VMEM((depth, width), jnp.bfloat16),
            f32(nodes, nz, nx * piece, width),
            f32(nodes, nz, max(nx - 1, 1), piece, width),
            f32(nodes, max(nz - 1, 1), piece, width),
            f32(nodes, piece, width),
            *total_refs(early),
            *total_refs(1),
            pltpu.SemaphoreType.DMA((copies,)),
            pltpu.SemaphoreType.DMA((copies,)),
            pltpu.SemaphoreType.DMA,
        ],
        compiler_params=pltpu.CompilerParams(
            collective_id=0, has_side_effects=True, vmem_limit_bytes=61 * 1024 * 1024
        ),
    )(trailing_inverse, factor_cols, factor_blocks, diag_inverse)


def solution(mesh):
    return jax.shard_map(
        per_device,
        mesh=mesh,
        in_specs=(P("row", "col"), P(None, ("col", "row"), None), P(), P()),
        out_specs=(P(None, ("row", "col"), None), P(), P()),
        check_vma=False,
    )
```
